32 devices in a mesh: dp: 4 (over y, core), tensor: 8 (over z, x).
Axes of the slice: x: 2, y: 2, z: 4, core: 2. Of those that a mesh axis runs over, the one named last changes fastest.
Arguments:
- tokens: bfloat16 [1408, 4096], P('dp', 'tensor'), may hold values from -6 to 6
- grad_out: bfloat16 [1408, 4096], P('dp', 'tensor'), may hold values from -6 to 6
- routes: float32 [4, 2, 16], P('dp'), may hold values from 0.005 to 0.3
- counts: int32 [4], P('dp'), may hold values from 176 to 352
- up_weight: bfloat16 [16, 4096, 4096], P(None, 'dp', 'tensor'), may hold values from -0.09375 to 0.09375
- down_weight: bfloat16 [16, 4096, 4096], P(None, 'tensor', 'dp'), may hold values from -0.09375 to 0.09375
Outputs:
- input_grad: bfloat16 [1408, 4096], P('dp', 'tensor')
- up_grad: bfloat16 [16, 4096, 4096], P(None, 'dp', 'tensor')
- down_grad: bfloat16 [16, 4096, 4096], P(None, 'tensor', 'dp')
- route_grad: float32 [4, 2, 16], P('dp')
The draws below stay inside these ranges and needn't reach their ends.
Inputs may be any that keep to these rules, and one draw needn't show every extreme that they name: `counts`: the valid tokens of a data group, at least one whole segment.
All inputs are finite; a program needn't handle non-finite values.
Results may differ from the reference program's by a relative error of at most 0.02.
Values may be sent and summed in bfloat16 or wider, within the bound.
A program may use at most 192 MiB of HBM per device.

```python
import math
import jax
import jax.numpy as jnp
from jax import lax

D = 4096
FFN = 4096
EXPERTS = 16
SEGS = 2
SEG_LEN = 176
TOK_GROUP = 352
GROUPS = 4
TOKENS = 1408
N_DP = 4
N_TENSOR = 8


def touch_ends(entries, key, least, high):
    index_at = [jax.random.randint(jax.random.fold_in(key, axis), (), 0, length) for axis, length in enumerate(entries.shape)]
    longest = entries.shape.index(max(entries.shape))
    beside = index_at[:longest] + [(index_at[longest] + 1) % entries.shape[longest]] + index_at[longest + 1:]
    return entries.at[tuple(index_at)].set(least).at[tuple(beside)].set(high)


def level_of(key, extent, pieces, low, high):
    def one(position, shards_of):
        heights = jax.random.uniform(jax.random.fold_in(jax.random.fold_in(key, 6), position), (shards_of,), jnp.float32, low / len(pieces), high / len(pieces))
        return jnp.repeat(jnp.exp(heights), extent[position] // shards_of).reshape((-1,) + (1,) * (len(extent) - position - 1))

    factor_of = one(*pieces[0])
    for cut in pieces[1:]:
        factor_of = factor_of * one(*cut)
    return factor_of


def bell_draw(own_key, extent, scale, limit, split=(), held_as=jnp.bfloat16):
    level = level_of(own_key, extent, split, -0.22, 0.18) if split else 1.0
    values = jax.random.normal(own_key, extent, jnp.float32) * scale * level
    return jnp.minimum(jnp.maximum(values, -limit), limit).astype(held_as)


def setup_inputs(seed: int = 0) -> dict:
    arg_keys = jax.random.split(jax.random.key(seed), 7)
    tokens = bell_draw(arg_keys[0], (TOKENS, D), 1.0, 6.0, ((0, 4), (1, 8)))
    grad_out = bell_draw(arg_keys[1], (TOKENS, D), 1.0, 6.0, ((0, 4), (1, 8)))
    routes = jnp.clip(jnp.exp(math.log(0.3) - 4.0943446 * jax.random.uniform(arg_keys[2], (GROUPS, SEGS, EXPERTS), jnp.float32) ** level_of(arg_keys[2], (GROUPS, SEGS, EXPERTS), ((0, 4),), -0.2, 0.2)), 0.005, 0.3)
    counts = touch_ends(jax.random.randint(arg_keys[3], (GROUPS,), SEG_LEN, TOK_GROUP + 1), jax.random.fold_in(arg_keys[3], 1), SEG_LEN, TOK_GROUP).astype(jnp.int32)
    up_weight = bell_draw(arg_keys[4], (EXPERTS, D, FFN), D ** -0.5, 0.09375, ((1, 4), (2, 8)))
    down_weight = bell_draw(arg_keys[5], (EXPERTS, FFN, D), FFN ** -0.5, 0.09375, ((1, 8), (2, 4)))
    return dict(tokens=tokens, grad_out=grad_out, routes=routes, counts=counts, up_weight=up_weight, down_weight=down_weight)


gelu_scale = 0.7978845608
gelu_cubic = 0.044715


def gelu_pair(inputs):
    inner = gelu_scale * (inputs + gelu_cubic * inputs * inputs * inputs)
    tangent = jnp.tanh(inner)
    activated = 0.5 * inputs * (1.0 + tangent)
    derivative = 0.5 * (1.0 + tangent) + 0.5 * inputs * (1.0 - tangent * tangent) * gelu_scale * (1.0 + 3.0 * gelu_cubic * inputs * inputs)
    return activated, derivative


def reference(tokens, grad_out, routes, counts, up_weight, down_weight):
    experts, width, hidden = up_weight.shape
    segments = routes.shape[1]
    group_rows = tokens.shape[0] // N_DP
    seg_rows = group_rows // segments
    slices = N_TENSOR
    up_flat = up_weight.reshape(experts, -1)
    down_flat = down_weight.reshape(experts, -1)
    up_wide = up_flat.astype(jnp.float32)
    down_wide = down_flat.astype(jnp.float32)
    high = lax.Precision.HIGHEST

    def per_group(carry, group):
        up_acc, down_acc = carry
        start = (group * group_rows).astype(jnp.int32)
        group_tokens = lax.dynamic_slice_in_dim(tokens, start, group_rows, 0)
        group_grads = lax.dynamic_slice_in_dim(grad_out, start, group_rows, 0)
        valid = (jnp.arange(group_rows, dtype=jnp.int32) < counts[group])[:, None]
        group_grads = jnp.where(valid, group_grads, jnp.zeros_like(group_grads))
        weights = routes[group]
        merged_up = jnp.dot(weights, up_wide, precision=high).reshape(segments, width, hidden).astype(jnp.bfloat16)
        merged_down = jnp.dot(weights, down_wide, precision=high).reshape(segments, hidden, width).astype(jnp.bfloat16)
        input_parts = []
        products = []
        for segment in range(segments):
            seg_tokens = group_tokens[segment * seg_rows:(segment + 1) * seg_rows]
            seg_grads = group_grads[segment * seg_rows:(segment + 1) * seg_rows]
            pre = jnp.dot(seg_tokens, merged_up[segment], preferred_element_type=jnp.float32)
            activated, derivative = gelu_pair(pre)
            activated = activated.astype(jnp.bfloat16)
            back = jnp.dot(seg_grads, merged_down[segment].T, preferred_element_type=jnp.float32)
            hidden_grad = (back * derivative).astype(jnp.bfloat16)
            up_term = jnp.dot(seg_tokens.T, hidden_grad, preferred_element_type=jnp.float32).astype(jnp.bfloat16)
            down_term = jnp.dot(activated.T, seg_grads, preferred_element_type=jnp.float32).astype(jnp.bfloat16)
            left_side = hidden_grad.astype(jnp.float32).reshape(seg_rows, slices, hidden // slices)
            right_side = merged_up[segment].astype(jnp.float32).reshape(width, slices, hidden // slices)
            partial_value = jnp.einsum('rth,dth->trd', left_side, right_side, precision=high).astype(jnp.bfloat16)
            partial_value = lax.optimization_barrier(partial_value)
            input_parts.append(jnp.sum(partial_value.astype(jnp.float32), axis=0).astype(jnp.bfloat16))
            up_vector = up_term.reshape(-1)
            down_vector = down_term.reshape(-1)
            up_acc = up_acc + weights[segment][:, None] * up_vector.astype(jnp.float32)[None, :]
            down_acc = down_acc + weights[segment][:, None] * down_vector.astype(jnp.float32)[None, :]
            inner_up = jnp.dot(up_flat, up_vector, preferred_element_type=jnp.float32)
            inner_down = jnp.dot(down_flat, down_vector, preferred_element_type=jnp.float32)
            products.append(inner_up + inner_down)
        return (up_acc, down_acc), (jnp.concatenate(input_parts, axis=0), jnp.stack(products, axis=0))

    start_acc = (jnp.zeros((experts, width * hidden), jnp.float32), jnp.zeros((experts, width * hidden), jnp.float32))
    (up_acc, down_acc), (input_rows, route_rows) = lax.scan(per_group, start_acc, jnp.arange(N_DP, dtype=jnp.int32))
    input_grad = input_rows.reshape(N_DP * group_rows, width)
    up_grad = up_acc.reshape(experts, width, hidden).astype(jnp.bfloat16)
    down_grad = down_acc.reshape(experts, hidden, width).astype(jnp.bfloat16)
    return (input_grad, up_grad, down_grad, route_rows)
```

```python
import jax
import jax.numpy as jnp
from jax import lax
from jax.experimental import pallas as pl
from jax.experimental.pallas import tpu as pltpu
from jax.sharding import PartitionSpec as P

gelu_scale = 0.7978845608
gelu_cubic = 0.044715
sub = 16
params = pltpu.CompilerParams(vmem_limit_bytes=48 * 1024 * 1024)


def gelu_pair(inputs):
    inner = gelu_scale * (inputs + gelu_cubic * inputs * inputs * inputs)
    tangent = jnp.tanh(inner)
    activated = 0.5 * inputs * (1.0 + tangent)
    derivative = 0.5 * (1.0 + tangent) + 0.5 * inputs * (1.0 - tangent * tangent) * gelu_scale * (
        1.0 + 3.0 * gelu_cubic * inputs * inputs
    )
    return (activated, derivative)


def spread(table):
    full = jnp.kron(table, jnp.eye(sub, dtype=jnp.float32))
    high = lax.reduce_precision(full, 8, 7)
    return high.astype(jnp.bfloat16), (full - high).astype(jnp.bfloat16)


def merge_kernel(mix_ref, weight_ref, out_ref):
    experts, rows, cols = weight_ref.shape
    count = out_ref.shape[0]
    for part in range(rows // sub):
        span = slice(part * sub, (part + 1) * sub)
        block = weight_ref[:, span, :].reshape(experts * sub, cols)
        both = jnp.dot(mix_ref[...], block, preferred_element_type=jnp.float32)
        total = both[: count * sub] + both[count * sub :]
        out_ref[:, span, :] = total.reshape(count, sub, cols).astype(jnp.bfloat16)


def merge(mix, weight, count):
    experts, rows, cols = weight.shape
    step = min(rows, 128)
    return pl.pallas_call(
        merge_kernel,
        grid=(rows // step,),
        in_specs=[
            pl.BlockSpec(mix.shape, lambda b: (0, 0)),
            pl.BlockSpec((experts, step, cols), lambda b: (0, b, 0)),
        ],
        out_specs=pl.BlockSpec((count, step, cols), lambda b: (0, b, 0)),
        out_shape=jax.ShapeDtypeStruct((count, rows, cols), jnp.bfloat16),
        compiler_params=params,
        cost_estimate=pl.CostEstimate(
            flops=4 * count * sub * experts * rows * cols,
            bytes_accessed=2 * (experts + count) * rows * cols,
            transcendentals=0,
        ),
        name="merge",
    )(mix, weight)


def partial_kernel(turned, act_ref, weight_ref, out_ref, total_ref):
    part = pl.program_id(1)
    dims = (((1,), (1,)), ((), ())) if turned else (((1,), (0,)), ((), ()))
    term = lax.dot_general(act_ref[...], weight_ref[...], dims, preferred_element_type=jnp.float32)

    @pl.when(part == 0)
    def _():
        total_ref[...] = term

    @pl.when(part > 0)
    def _():
        total_ref[...] += term

    @pl.when(part == pl.num_programs(1) - 1)
    def _():
        out_ref[...] = total_ref[...].astype(out_ref.dtype)


def partial_product(acts, weight, turned):
    groups, parts, segments, rows, width = acts.shape
    count = groups * segments
    hidden = weight.shape[1] if turned else weight.shape[2]
    weight_spec = (
        pl.BlockSpec((None, hidden, width), lambda k, c: (k, 0, c))
        if turned
        else pl.BlockSpec((None, width, hidden), lambda k, c: (k, c, 0))
    )
    return pl.pallas_call(
        lambda *refs: partial_kernel(turned, *refs),
        grid=(count, parts),
        in_specs=[
            pl.BlockSpec(
                (None, None, None, rows, width),
                lambda k, c: (k // segments, c, k % segments, 0, 0),
            ),
            weight_spec,
        ],
        out_specs=pl.BlockSpec((None, rows, hidden), lambda k, c: (k, 0, 0)),
        out_shape=jax.ShapeDtypeStruct((count, rows, hidden), jnp.bfloat16),
        scratch_shapes=[pltpu.VMEM((rows, hidden), jnp.float32)],
        compiler_params=params,
        cost_estimate=pl.CostEstimate(
            flops=2 * count * parts * rows * width * hidden,
            bytes_accessed=2 * weight.size + 2 * acts.size,
            transcendentals=0,
        ),
        name="partial_product",
    )(acts, weight)


def input_kernel(grad_ref, weight_ref, out_ref):
    out_ref[...] = lax.dot_general(
        grad_ref[...], weight_ref[...], (((1,), (1,)), ((), ())),
        preferred_element_type=jnp.float32,
    ).astype(out_ref.dtype)


def input_product(grads, weight, groups, parts, segments):
    count, rows, hidden = grads.shape
    width = weight.shape[1] // parts
    return pl.pallas_call(
        input_kernel,
        grid=(count, parts),
        in_specs=[
            pl.BlockSpec((None, rows, hidden), lambda k, c: (k, 0, 0)),
            pl.BlockSpec((None, width, hidden), lambda k, c: (k, c, 0)),
        ],
        out_specs=pl.BlockSpec(
            (None, None, None, rows, width),
            lambda k, c: (k // segments, c, k % segments, 0, 0),
        ),
        out_shape=jax.ShapeDtypeStruct((groups, parts, segments, rows, width), jnp.bfloat16),
        compiler_params=params,
        cost_estimate=pl.CostEstimate(
            flops=2 * weight.size * rows,
            bytes_accessed=2 * weight.size + 4 * grads.size,
            transcendentals=0,
        ),
        name="input_product",
    )(grads, weight)


def grad_kernel(segments, mix_ref, left_ref, right_ref, weight_ref, out_ref, inner_ref, term_ref):
    experts, rows, cols = weight_ref.shape
    groups, parts, group_rows, width = right_ref.shape
    seg_rows = group_rows // segments
    count = groups * segments

    @pl.when(pl.program_id(0) == 0)
    def _():
        inner_ref[...] = jnp.zeros_like(inner_ref)

    for k in range(count):
        span = slice((k % segments) * seg_rows, (k % segments + 1) * seg_rows)
        left = left_ref[k // segments, span, :]
        for part in range(parts):
            term = lax.dot_general(
                left, right_ref[k // segments, part, span, :], (((0,), (0,)), ((), ())),
                preferred_element_type=jnp.float32,
            )
            term_ref[k, :, part * width : (part + 1) * width] = term.astype(jnp.bfloat16)
    for part in range(rows // sub):
        span = slice(part * sub, (part + 1) * sub)
        terms = term_ref[:, span, :].reshape(count * sub, cols)
        weights = weight_ref[:, span, :].reshape(experts * sub, cols)
        inner_ref[...] += lax.dot_general(
            terms, weights, (((1,), (1,)), ((), ())), preferred_element_type=jnp.float32
        )
        total = jnp.dot(
            mix_ref[...], jnp.concatenate([terms, terms], axis=0),
            preferred_element_type=jnp.float32,
        )
        out_ref[:, span, :] = total.reshape(experts, sub, cols).astype(jnp.bfloat16)


def expert_grads(mix, left, right, weight, segments):
    experts, rows, cols = weight.shape
    groups, pieces, group_rows, left_width = left.shape
    count = groups * segments
    step = 128
    per = left_width // step
    return pl.pallas_call(
        lambda *refs: grad_kernel(segments, *refs),
        grid=(rows // step,),
        in_specs=[
            pl.BlockSpec(mix.shape, lambda b: (0, 0)),
            pl.BlockSpec(
                (groups, None, group_rows, step), lambda b: (0, b // per, 0, b % per)
            ),
            pl.BlockSpec(right.shape, lambda b: (0, 0, 0, 0)),
            pl.BlockSpec((experts, step, cols), lambda b: (0, b, 0)),
        ],
        out_specs=[
            pl.BlockSpec((experts, step, cols), lambda b: (0, b, 0)),
            pl.BlockSpec((count * sub, experts * sub), lambda b: (0, 0)),
        ],
        out_shape=[
            jax.ShapeDtypeStruct(weight.shape, jnp.bfloat16),
            jax.ShapeDtypeStruct((count * sub, experts * sub), jnp.float32),
        ],
        scratch_shapes=[pltpu.VMEM((count, step, cols), jnp.bfloat16)],
        compiler_params=params,
        cost_estimate=pl.CostEstimate(
            flops=2 * rows * cols * groups * group_rows + 6 * count * sub * experts * rows * cols,
            bytes_accessed=4 * weight.size + 2 * left.size + 2 * right.size,
            transcendentals=0,
        ),
        name="expert_grads",
    )(mix, left, right, weight)


def make_body(n_dp, n_tensor):
    parts = n_tensor // n_dp
    both = ("dp", "tensor")
    moves = []
    for i in range(n_dp):
        for a in range(n_dp):
            for b in range(parts):
                moves.append((i * n_tensor + parts * a + b, a * n_tensor + parts * i + b))
    returns = [(target, source) for source, target in moves]

    def body(tokens, grad_out, routes, counts, up_weight, down_weight):
        group_rows, width = tokens.shape
        experts = up_weight.shape[0]
        segments = routes.shape[1]
        seg_rows = group_rows // segments
        hidden = up_weight.shape[2]
        count = n_dp * segments
        valid = (jnp.arange(group_rows, dtype=jnp.int32) < counts[0])[:, None]
        masked = jnp.where(valid, grad_out, jnp.zeros_like(grad_out))
        moved_tokens = lax.ppermute(tokens, both, moves)
        moved_grads = lax.ppermute(masked, both, moves)
        all_tokens = lax.all_gather(moved_tokens, "tensor", axis=0, tiled=False)
        all_grads = lax.all_gather(moved_grads, "tensor", axis=0, tiled=False)
        all_tokens = all_tokens.reshape(n_dp, parts, group_rows, width)
        all_grads = all_grads.reshape(n_dp, parts, group_rows, width)
        split = (n_dp, parts, segments, seg_rows, width)

        all_routes = lax.all_gather(routes, "dp", axis=0, tiled=True)
        flat_routes = all_routes.reshape(-1, experts)
        mix_merge = jnp.concatenate(spread(flat_routes), axis=0)
        mix_grads = jnp.concatenate(spread(flat_routes.T), axis=1)
        merged_up = merge(mix_merge, up_weight, count)
        merged_down = merge(mix_merge, down_weight, count)

        pre_parts = partial_product(all_tokens.reshape(split), merged_up, False)
        pre_parts = lax.all_to_all(
            pre_parts.reshape(n_dp, group_rows, hidden), "dp", 0, 0, tiled=True
        )
        back_parts = partial_product(all_grads.reshape(split), merged_down, True)
        back_parts = lax.all_to_all(
            back_parts.reshape(n_dp, group_rows, hidden), "dp", 0, 0, tiled=True
        )
        pre = jnp.sum(pre_parts.astype(jnp.float32), axis=0)
        back = jnp.sum(back_parts.astype(jnp.float32), axis=0)
        activated, slope = gelu_pair(pre)
        hidden_grad = (back * slope).astype(jnp.bfloat16)
        all_act = lax.all_gather(activated.astype(jnp.bfloat16), "dp", axis=0, tiled=False)
        all_hidden = lax.all_gather(hidden_grad, "dp", axis=0, tiled=False)

        partials = input_product(
            all_hidden.reshape(count, seg_rows, hidden), merged_up, n_dp, parts, segments
        )
        summed = lax.psum_scatter(
            partials.reshape(n_tensor, group_rows, width), "tensor",
            scatter_dimension=0, tiled=False,
        )
        input_grad = lax.ppermute(summed, both, returns)

        up_grad, inner_up = expert_grads(
            mix_grads, all_tokens, all_hidden[:, None], up_weight, segments
        )
        down_grad, inner_down = expert_grads(
            mix_grads, all_act[:, None], all_grads, down_weight, segments
        )
        inner = (inner_up + inner_down).reshape(count, sub, experts, sub)
        table = jnp.einsum("kaea->ke", inner).reshape(all_routes.shape)
        totals = lax.psum(table, both)
        route_grad = lax.dynamic_slice_in_dim(totals, lax.axis_index("dp"), 1, 0)
        return (input_grad, up_grad, down_grad, route_grad)

    return body


def solution(mesh):
    return jax.shard_map(
        make_body(mesh.shape["dp"], mesh.shape["tensor"]),
        mesh=mesh,
        in_specs=(
            P("dp", "tensor"),
            P("dp", "tensor"),
            P("dp", None, None),
            P("dp"),
            P(None, "dp", "tensor"),
            P(None, "tensor", "dp"),
        ),
        out_specs=(
            P("dp", "tensor"),
            P(None, "dp", "tensor"),
            P(None, "tensor", "dp"),
            P("dp", None, None),
        ),
        check_vma=False,
    )
```

```python
import jax
import jax.numpy as jnp
from jax import lax
from jax.experimental import pallas as pl
from jax.experimental.pallas import tpu as pltpu
from jax.sharding import PartitionSpec as P

gelu_scale = 0.7978845608
gelu_cubic = 0.044715
sub = 16
params = pltpu.CompilerParams(vmem_limit_bytes=48 * 1024 * 1024)


def gelu_pair(inputs):
    inner = gelu_scale * (inputs + gelu_cubic * inputs * inputs * inputs)
    tangent = jnp.tanh(inner)
    activated = 0.5 * inputs * (1.0 + tangent)
    derivative = 0.5 * (1.0 + tangent) + 0.5 * inputs * (1.0 - tangent * tangent) * gelu_scale * (
        1.0 + 3.0 * gelu_cubic * inputs * inputs
    )
    return (activated, derivative)


def spread(table):
    full = jnp.kron(table, jnp.eye(sub, dtype=jnp.float32))
    high = lax.reduce_precision(full, 8, 7)
    return high.astype(jnp.bfloat16), (full - high).astype(jnp.bfloat16)


def merge_kernel(mix_ref, weight_ref, out_ref):
    experts, rows, cols = weight_ref.shape
    count = out_ref.shape[0]
    for part in range(rows // sub):
        span = slice(part * sub, (part + 1) * sub)
        block = weight_ref[:, span, :].reshape(experts * sub, cols)
        both = jnp.dot(mix_ref[...], block, preferred_element_type=jnp.float32)
        total = both[: count * sub] + both[count * sub :]
        out_ref[:, span, :] = total.reshape(count, sub, cols).astype(jnp.bfloat16)


def merge(mix, weight, count):
    experts, rows, cols = weight.shape
    step = min(rows, 128)
    return pl.pallas_call(
        merge_kernel,
        grid=(rows // step,),
        in_specs=[
            pl.BlockSpec(mix.shape, lambda b: (0, 0)),
            pl.BlockSpec((experts, step, cols), lambda b: (0, b, 0)),
        ],
        out_specs=pl.BlockSpec((count, step, cols), lambda b: (0, b, 0)),
        out_shape=jax.ShapeDtypeStruct((count, rows, cols), jnp.bfloat16),
        compiler_params=params,
        cost_estimate=pl.CostEstimate(
            flops=4 * count * sub * experts * rows * cols,
            bytes_accessed=2 * (experts + count) * rows * cols,
            transcendentals=0,
        ),
        name="merge",
    )(mix, weight)


def partial_kernel(turned, act_ref, weight_ref, out_ref, total_ref):
    part = pl.program_id(1)
    dims = (((1,), (1,)), ((), ())) if turned else (((1,), (0,)), ((), ()))
    term = lax.dot_general(act_ref[...], weight_ref[...], dims, preferred_element_type=jnp.float32)

    @pl.when(part == 0)
    def _():
        total_ref[...] = term

    @pl.when(part > 0)
    def _():
        total_ref[...] += term

    @pl.when(part == pl.num_programs(1) - 1)
    def _():
        out_ref[...] = total_ref[...].astype(out_ref.dtype)


def partial_product(acts, weight, turned):
    groups, parts, segments, rows, width = acts.shape
    count = groups * segments
    hidden = weight.shape[1] if turned else weight.shape[2]
    weight_spec = (
        pl.BlockSpec((None, hidden, width), lambda k, c: (k, 0, c))
        if turned
        else pl.BlockSpec((None, width, hidden), lambda k, c: (k, c, 0))
    )
    return pl.pallas_call(
        lambda *refs: partial_kernel(turned, *refs),
        grid=(count, parts),
        in_specs=[
            pl.BlockSpec(
                (None, None, None, rows, width),
                lambda k, c: (k // segments, c, k % segments, 0, 0),
            ),
            weight_spec,
        ],
        out_specs=pl.BlockSpec((None, rows, hidden), lambda k, c: (k, 0, 0)),
        out_shape=jax.ShapeDtypeStruct((count, rows, hidden), jnp.bfloat16),
        scratch_shapes=[pltpu.VMEM((rows, hidden), jnp.float32)],
        compiler_params=params,
        cost_estimate=pl.CostEstimate(
            flops=2 * count * parts * rows * width * hidden,
            bytes_accessed=2 * weight.size + 2 * acts.size,
            transcendentals=0,
        ),
        name="partial_product",
    )(acts, weight)


def input_kernel(grad_ref, weight_ref, out_ref):
    out_ref[...] = lax.dot_general(
        grad_ref[...], weight_ref[...], (((1,), (1,)), ((), ())),
        preferred_element_type=jnp.float32,
    ).astype(out_ref.dtype)


def input_product(grads, weight, groups, parts, segments):
    count, rows, hidden = grads.shape
    width = weight.shape[1] // parts
    return pl.pallas_call(
        input_kernel,
        grid=(count, parts),
        in_specs=[
            pl.BlockSpec((None, rows, hidden), lambda k, c: (k, 0, 0)),
            pl.BlockSpec((None, width, hidden), lambda k, c: (k, c, 0)),
        ],
        out_specs=pl.BlockSpec(
            (None, None, None, rows, width),
            lambda k, c: (k // segments, c, k % segments, 0, 0),
        ),
        out_shape=jax.ShapeDtypeStruct((groups, parts, segments, rows, width), jnp.bfloat16),
        compiler_params=params,
        cost_estimate=pl.CostEstimate(
            flops=2 * weight.size * rows,
            bytes_accessed=2 * weight.size + 4 * grads.size,
            transcendentals=0,
        ),
        name="input_product",
    )(grads, weight)


def grad_kernel(segments, mix_ref, left_ref, right_ref, weight_ref, out_ref, inner_ref, term_ref):
    experts, rows, cols = weight_ref.shape
    groups, parts, group_rows, width = right_ref.shape
    seg_rows = group_rows // segments
    count = groups * segments

    @pl.when(pl.program_id(0) == 0)
    def _():
        inner_ref[...] = jnp.zeros_like(inner_ref)

    for k in range(count):
        span = slice((k % segments) * seg_rows, (k % segments + 1) * seg_rows)
        left = left_ref[k // segments, span, :]
        for part in range(parts):
            term = lax.dot_general(
                left, right_ref[k // segments, part, span, :], (((0,), (0,)), ((), ())),
                preferred_element_type=jnp.float32,
            )
            term_ref[k, :, part * width : (part + 1) * width] = term.astype(jnp.bfloat16)
    for part in range(rows // sub):
        span = slice(part * sub, (part + 1) * sub)
        terms = term_ref[:, span, :].reshape(count * sub, cols)
        weights = weight_ref[:, span, :].reshape(experts * sub, cols)
        inner_ref[...] += lax.dot_general(
            terms, weights, (((1,), (1,)), ((), ())), preferred_element_type=jnp.float32
        )
        total = jnp.dot(
            mix_ref[...], jnp.concatenate([terms, terms], axis=0),
            preferred_element_type=jnp.float32,
        )
        out_ref[:, span, :] = total.reshape(experts, sub, cols).astype(jnp.bfloat16)


def expert_grads(mix, left, right, weight, segments):
    experts, rows, cols = weight.shape
    groups, pieces, group_rows, left_width = left.shape
    count = groups * segments
    step = 128
    per = left_width // step
    return pl.pallas_call(
        lambda *refs: grad_kernel(segments, *refs),
        grid=(rows // step,),
        in_specs=[
            pl.BlockSpec(mix.shape, lambda b: (0, 0)),
            pl.BlockSpec(
                (groups, None, group_rows, step), lambda b: (0, b // per, 0, b % per)
            ),
            pl.BlockSpec(right.shape, lambda b: (0, 0, 0, 0)),
            pl.BlockSpec((experts, step, cols), lambda b: (0, b, 0)),
        ],
        out_specs=[
            pl.BlockSpec((experts, step, cols), lambda b: (0, b, 0)),
            pl.BlockSpec((count * sub, experts * sub), lambda b: (0, 0)),
        ],
        out_shape=[
            jax.ShapeDtypeStruct(weight.shape, jnp.bfloat16),
            jax.ShapeDtypeStruct((count * sub, experts * sub), jnp.float32),
        ],
        scratch_shapes=[pltpu.VMEM((count, step, cols), jnp.bfloat16)],
        compiler_params=params,
        cost_estimate=pl.CostEstimate(
            flops=2 * rows * cols * groups * group_rows + 6 * count * sub * experts * rows * cols,
            bytes_accessed=4 * weight.size + 2 * left.size + 2 * right.size,
            transcendentals=0,
        ),
        name="expert_grads",
    )(mix, left, right, weight)


def make_body(n_dp, n_tensor):
    parts = n_tensor // n_dp
    both = ("dp", "tensor")
    moves = []
    for i in range(n_dp):
        for a in range(n_dp):
            for b in range(parts):
                moves.append((i * n_tensor + parts * a + b, a * n_tensor + parts * i + b))
    returns = [(target, source) for source, target in moves]

    def body(tokens, grad_out, routes, counts, up_weight, down_weight):
        group_rows, width = tokens.shape
        experts = up_weight.shape[0]
        segments = routes.shape[1]
        seg_rows = group_rows // segments
        hidden = up_weight.shape[2]
        count = n_dp * segments
        valid = (jnp.arange(group_rows, dtype=jnp.int32) < counts[0])[:, None]
        masked = jnp.where(valid, grad_out, jnp.zeros_like(grad_out))
        moved_tokens = lax.ppermute(tokens, both, moves)
        moved_grads = lax.ppermute(masked, both, moves)
        all_tokens = lax.all_gather(moved_tokens, "tensor", axis=0, tiled=False)
        all_grads = lax.all_gather(moved_grads, "tensor", axis=0, tiled=False)
        all_tokens = all_tokens.reshape(n_dp, parts, group_rows, width)
        all_grads = all_grads.reshape(n_dp, parts, group_rows, width)
        split = (n_dp, parts, segments, seg_rows, width)

        all_routes = lax.all_gather(routes, "dp", axis=0, tiled=True)
        flat_routes = all_routes.reshape(-1, experts)
        mix_merge = jnp.concatenate(spread(flat_routes), axis=0)
        mix_grads = jnp.concatenate(spread(flat_routes.T), axis=1)
        merged_up = merge(mix_merge, up_weight, count)
        merged_down = merge(mix_merge, down_weight, count)

        pre_parts = partial_product(all_tokens.reshape(split), merged_up, False)
        pre_parts = lax.all_to_all(
            pre_parts.reshape(n_dp, group_rows, hidden), "dp", 0, 0, tiled=True
        )
        back_parts = partial_product(all_grads.reshape(split), merged_down, True)
        back_parts = lax.all_to_all(
            back_parts.reshape(n_dp, group_rows, hidden), "dp", 0, 0, tiled=True
        )
        pre = jnp.sum(pre_parts.astype(jnp.float32), axis=0)
        back = jnp.sum(back_parts.astype(jnp.float32), axis=0)
        activated, slope = gelu_pair(pre)
        hidden_grad = (back * slope).astype(jnp.bfloat16)
        pair = jnp.stack([activated.astype(jnp.bfloat16), hidden_grad], axis=0)
        all_pair = lax.all_gather(pair, "dp", axis=0, tiled=False)
        all_act, all_hidden = all_pair[:, 0], all_pair[:, 1]

        partials = input_product(
            all_hidden.reshape(count, seg_rows, hidden), merged_up, n_dp, parts, segments
        )
        summed = lax.psum_scatter(
            partials.reshape(n_tensor, group_rows, width), "tensor",
            scatter_dimension=0, tiled=False,
        )
        input_grad = lax.ppermute(summed, both, returns)

        up_grad, inner_up = expert_grads(
            mix_grads, all_tokens, all_hidden[:, None], up_weight, segments
        )
        down_grad, inner_down = expert_grads(
            mix_grads, all_act[:, None], all_grads, down_weight, segments
        )
        inner = (inner_up + inner_down).reshape(count, sub, experts, sub)
        table = jnp.einsum("kaea->ke", inner).reshape(all_routes.shape)
        totals = lax.psum(table, both)
        route_grad = lax.dynamic_slice_in_dim(totals, lax.axis_index("dp"), 1, 0)
        return (input_grad, up_grad, down_grad, route_grad)

    return body


def solution(mesh):
    return jax.shard_map(
        make_body(mesh.shape["dp"], mesh.shape["tensor"]),
        mesh=mesh,
        in_specs=(
            P("dp", "tensor"),
            P("dp", "tensor"),
            P("dp", None, None),
            P("dp"),
            P(None, "dp", "tensor"),
            P(None, "tensor", "dp"),
        ),
        out_specs=(
            P("dp", "tensor"),
            P(None, "dp", "tensor"),
            P(None, "tensor", "dp"),
            P("dp", None, None),
        ),
        check_vma=False,
    )
```
